768 devices in a mesh: band: 24 (over z, y_hi), ga: 32 (over x, y_lo, core).
Axes of the slice: x: 4, y: 8 (y_hi: 2, y_lo: 4; y = y_hi * 4 + y_lo), z: 12, core: 2. Of those that a mesh axis runs over, the one named last changes fastest.
Arguments:
- pair_dens: bfloat16 [24, 48, 36864], P('band', None, 'ga'), may hold values from -0.03125 to 0.03125
- energies: float32 [24], P('band'), may hold values from -2 to 2
- freq_index: int32 [1], replicated, may hold values from 0 to 15
- screened: bfloat16 [24, 32, 48, 36864], P('band', None, None, 'ga'), may hold values from -6 to 6
Outputs:
- sigma: float32 [48, 48], P('band')
The draws below stay inside these ranges and needn't reach their ends.
All inputs are finite; a program needn't handle non-finite values.
Results may differ from the reference program's by a relative error of at most 0.012.
Values may be sent and summed in bfloat16 or wider, within the bound.
No kernel may reach another device: no remote copies, remote signals or barrier semaphores. Data moves between devices by JAX's collectives and lax.ppermute only.
A program may use at most 64 MiB of HBM per device.

```python
import jax
import jax.numpy as jnp
from jax import lax

NB = 48
NFREQ = 16
MB = 24
NG = 36864
SUB = 48
N_BAND = 24
N_GA = 32


def shard_levels(key, dims, cuts, low, high):
    gain, own = 1.0, jax.random.fold_in(key, 6)
    for position, shards_of in cuts:
        steps = jnp.exp(jax.random.uniform(jax.random.fold_in(own, position), (shards_of,), jnp.float32, low / len(cuts), high / len(cuts)))
        gain = gain * jnp.repeat(steps, dims[position] // shards_of).reshape([-1 if axis == position else 1 for axis in range(len(dims))])
    return gain


def scatter_about(stream_key, extent, spread, bound, cuts=(), held_as=jnp.bfloat16):
    values = spread * jax.random.normal(stream_key, extent, jnp.float32)
    if cuts:
        values = values * shard_levels(stream_key, extent, cuts, -0.22, 0.18)
    return jnp.clip(values, -bound, bound).astype(held_as)


def setup_inputs(seed: int = 0) -> dict:
    seeds = jax.random.split(jax.random.key(seed), 5)
    return {
        "pair_dens": scatter_about(seeds[0], (MB, NB, NG), NG ** -0.5, 0.03125, ((0, 24), (2, 32))),
        "energies": jnp.clip(jax.random.uniform(seeds[1], (MB,), jnp.float32, -2.0, 2.0) * shard_levels(seeds[1], (MB,), ((0, 24),), -0.4, 0.0), -2.0, 2.0),
        "freq_index": jax.random.randint(seeds[2], (1,), 0, NFREQ).astype(jnp.int32),
        "screened": scatter_about(seeds[3], (N_BAND, N_GA, SUB, NG), 1.0, 6.0, ((0, 24), (3, 32))),
    }


def reference(pair_dens, energies, freq_index, screened):
    mcount, nbands, nwaves = pair_dens.shape
    nband_groups, nga_groups, subrows, _ = screened.shape
    split = pair_dens.reshape(mcount, nbands, nga_groups, nband_groups, subrows)

    def add_group(total, group):
        rows = lax.dynamic_index_in_dim(split, group, 3, keepdims=False).reshape(mcount * nbands, nga_groups * subrows)
        block = lax.dynamic_index_in_dim(screened, group, 0, keepdims=False).reshape(nga_groups * subrows, nwaves)
        return total + jnp.dot(rows, block, preferred_element_type=jnp.float32), None

    proj, _ = lax.scan(add_group, jnp.zeros((mcount * nbands, nwaves), jnp.float32), jnp.arange(nband_groups, dtype=jnp.int32))
    proj = proj.reshape(mcount, nbands, nwaves)
    omega = 0.1 * jnp.exp(jnp.log(20.0) * freq_index[0].astype(jnp.float32) / (NFREQ - 1))
    coef = energies / (energies * energies + omega * omega)
    weighted = (proj * coef[:, None, None]).astype(jnp.bfloat16)
    return jnp.einsum("mng,mpg->np", weighted.astype(jnp.float32), pair_dens.astype(jnp.float32), precision=lax.Precision.HIGHEST)
```

```python
import jax
import jax.numpy as jnp
from jax import lax
from jax.experimental import pallas as pl
from jax.experimental.pallas import tpu as pltpu
from jax.sharding import Mesh
from jax.sharding import PartitionSpec as P

NFREQ = 16
Z, YH, X, YL, CORE = 12, 2, 4, 4, 2
BAND = ("z", "yh")
GA = ("x", "yl", "core")
GROUP = 8


def turn_kernel(core_ref, w_ref, out_ref):
    core = core_ref[0]
    half = out_ref.shape[1] // 2
    for side in range(2):
        owner = jnp.where(side == 0, core, 1 - core)
        rows = jnp.concatenate([w_ref[2 * i + owner] for i in range(X * YL)], axis=0)
        out_ref[:, side * half : (side + 1) * half] = rows.T


def proj_kernel(wt_ref, own_ref, other_ref, out_ref):
    half = own_ref.shape[0]
    total = jnp.dot(wt_ref[:, :half], own_ref[...], preferred_element_type=jnp.float32)
    total += jnp.dot(wt_ref[:, half:], other_ref[...], preferred_element_type=jnp.float32)
    out_ref[...] = total.astype(out_ref.dtype)


def sigma_kernel(cols_ref, proj_ref, out_ref):
    nb = out_ref.shape[0]
    width = GROUP * nb
    total = jnp.zeros((nb, nb), jnp.float32)
    for g in range(cols_ref.shape[0] // width):
        block = jnp.dot(
            cols_ref[g * width : (g + 1) * width, :],
            proj_ref[:, g * width : (g + 1) * width],
            preferred_element_type=jnp.float32,
        )
        for i in range(GROUP):
            total += block[i * nb : (i + 1) * nb, i * nb : (i + 1) * nb]
    out_ref[...] = total.T


def on_device(pair_dens, energies, freq_index, screened):
    mine = pair_dens[0]
    nb, width = mine.shape
    sub = width // (Z * YH)
    rowcount = X * YL * CORE * sub

    swapped = lax.ppermute(mine, "yh", [(0, 1), (1, 0)])
    first = lax.axis_index("yh") == 0
    both = jnp.stack([jnp.where(first, mine, swapped), jnp.where(first, swapped, mine)])
    cols = lax.all_gather(both, "z").reshape(Z * YH * nb, width)

    omega = 0.1 * jnp.exp(jnp.log(20.0) * freq_index[0].astype(jnp.float32) / (NFREQ - 1))
    coef = energies[0] / (energies[0] * energies[0] + omega * omega)
    scaled = (mine.astype(jnp.float32) * coef).astype(jnp.bfloat16)
    pieces = scaled.T.reshape(Z * YH, sub, nb)
    got = lax.all_to_all(pieces, BAND, 0, 0, tiled=True)
    rows = got.transpose(1, 0, 2).reshape(sub, Z * YH * nb)
    rows = lax.all_gather(rows, "yl", axis=0, tiled=True)
    rows = lax.all_gather(rows, "x", axis=0, tiled=True)
    other = lax.ppermute(rows, "core", [(0, 1), (1, 0)])

    core = lax.axis_index("core").astype(jnp.int32).reshape(1)
    turned = pl.pallas_call(
        turn_kernel,
        out_shape=jax.ShapeDtypeStruct((width, rowcount), jnp.bfloat16),
        in_specs=[pl.BlockSpec(memory_space=pltpu.SMEM), pl.BlockSpec(memory_space=pltpu.VMEM)],
        out_specs=pl.BlockSpec(memory_space=pltpu.VMEM),
        compiler_params=pltpu.CompilerParams(vmem_limit_bytes=40 << 20),
        cost_estimate=pl.CostEstimate(flops=0, bytes_accessed=4 * rowcount * width, transcendentals=0),
    )(core, screened[0])

    mcols = Z * YH * nb
    tile = GROUP * nb
    proj = pl.pallas_call(
        proj_kernel,
        grid=(mcols // tile,),
        out_shape=jax.ShapeDtypeStruct((width, mcols), jnp.bfloat16),
        in_specs=[
            pl.BlockSpec((width, rowcount), lambda j: (0, 0)),
            pl.BlockSpec((rowcount // 2, tile), lambda j: (0, j)),
            pl.BlockSpec((rowcount // 2, tile), lambda j: (0, j)),
        ],
        out_specs=pl.BlockSpec((width, tile), lambda j: (0, j)),
        compiler_params=pltpu.CompilerParams(vmem_limit_bytes=40 << 20),
        cost_estimate=pl.CostEstimate(
            flops=2 * width * mcols * rowcount, bytes_accessed=10 << 20, transcendentals=0
        ),
    )(turned, rows, other)

    part = pl.pallas_call(
        sigma_kernel,
        out_shape=jax.ShapeDtypeStruct((nb, nb), jnp.float32),
        in_specs=[pl.BlockSpec(memory_space=pltpu.VMEM)] * 2,
        out_specs=pl.BlockSpec(memory_space=pltpu.VMEM),
        compiler_params=pltpu.CompilerParams(vmem_limit_bytes=40 << 20),
        cost_estimate=pl.CostEstimate(
            flops=2 * width * mcols * tile, bytes_accessed=6 << 20, transcendentals=0
        ),
    )(cols, proj)

    share = nb // (Z * YH)
    part = lax.all_to_all(part.reshape(Z * YH, share, nb), BAND, 0, 0, tiled=True).sum(axis=0)
    spread = jnp.broadcast_to(part[None], (X * YL * CORE, share, nb))
    return lax.all_to_all(spread, GA, 0, 0, tiled=True).sum(axis=0)


def solution(mesh):
    fine = Mesh(mesh.devices.reshape(Z, YH, X, YL, CORE), BAND + GA)
    return jax.shard_map(
        on_device,
        mesh=fine,
        in_specs=(P(BAND, None, GA), P(BAND), P(), P(BAND, None, None, GA)),
        out_specs=P(BAND, None),
        check_vma=False,
    )
```

```python
import jax
import jax.numpy as jnp
from jax import lax
from jax.experimental import pallas as pl
from jax.experimental.pallas import tpu as pltpu
from jax.sharding import Mesh
from jax.sharding import PartitionSpec as P

NFREQ = 16
Z, YH, X, YL, CORE = 12, 2, 4, 4, 2
BAND = ("z", "yh")
GA = ("x", "yl", "core")
GROUP = 8
VMEM = pl.BlockSpec(memory_space=pltpu.VMEM)
SMEM = pl.BlockSpec(memory_space=pltpu.SMEM)
PARAMS = pltpu.CompilerParams(vmem_limit_bytes=40 << 20)


def order_kernel(pos_ref, w_ref, out_ref):
    sub = w_ref.shape[1]
    row = 0
    for step in range(X):
        x = lax.rem(pos_ref[0] + step, X)
        for side in range(CORE):
            core = pos_ref[1] if side == 0 else 1 - pos_ref[1]
            for yl in range(YL):
                out_ref[row : row + sub, :] = w_ref[(x * YL + yl) * CORE + core]
                row += sub


def pieces_kernel(pos_ref, coef_ref, both_ref, out_ref, turned_ref):
    scaled = [both_ref[i].astype(jnp.float32) * coef_ref[i] for i in range(YH)]
    turned_ref[...] = jnp.concatenate(scaled, axis=0).T.astype(turned_ref.dtype)
    sub = out_ref.shape[1]
    for z in range(Z):
        start = pl.multiple_of((z * YH + pos_ref[0]) * sub, sub)
        out_ref[z] = turned_ref[pl.ds(start, sub), :]


def rows_kernel(got_ref, out_ref):
    out_ref[...] = jnp.concatenate([got_ref[z] for z in range(Z)], axis=1)


def half_kernel(cols_ref, w_ref, out_ref):
    out_ref[...] = lax.dot_general(
        cols_ref[...], w_ref[...], (((1,), (1,)), ((), ())), preferred_element_type=jnp.float32
    ).astype(out_ref.dtype)


def sigma_kernel(half_ref, *refs):
    row_refs, out_ref = refs[:-1], refs[-1]
    nb = out_ref.shape[0]
    width = GROUP * nb
    depth = CORE * row_refs[0].shape[0]
    total = jnp.zeros((nb, nb), jnp.float32)
    for g in range(half_ref.shape[0] // width):
        span = slice(g * width, (g + 1) * width)
        block = jnp.zeros((width, width), jnp.float32)
        for step in range(X):
            rows = jnp.concatenate([r[:, span] for r in row_refs[CORE * step : CORE * step + CORE]], axis=0)
            block += jnp.dot(
                half_ref[span, step * depth : (step + 1) * depth],
                rows,
                preferred_element_type=jnp.float32,
            )
        for i in range(GROUP):
            total += block[i * nb : (i + 1) * nb, i * nb : (i + 1) * nb]
    out_ref[...] = total.T


def on_device(pair_dens, energies, freq_index, screened):
    mine = pair_dens[0]
    nb, width = mine.shape
    sub = width // (Z * YH)
    rowcount = X * YL * CORE * sub
    mcols = Z * YH * nb
    tile = GROUP * nb
    place = {axis: lax.axis_index(axis).astype(jnp.int32) for axis in ("yh", "x", "core")}
    swap = [(0, 1), (1, 0)]

    omega = 0.1 * jnp.exp(jnp.log(20.0) * freq_index[0].astype(jnp.float32) / (NFREQ - 1))
    coef = energies / (energies * energies + omega * omega)

    theirs = lax.ppermute(mine, "yh", swap)
    their_coef = lax.ppermute(coef, "yh", swap)
    both, their_coef = lax.optimization_barrier((jnp.stack([mine, theirs]), their_coef))
    cols = lax.all_gather(both, "z").reshape(mcols, width)

    ordered = pl.pallas_call(
        order_kernel,
        out_shape=jax.ShapeDtypeStruct((rowcount, width), jnp.bfloat16),
        in_specs=[SMEM, VMEM],
        out_specs=VMEM,
        compiler_params=PARAMS,
        cost_estimate=pl.CostEstimate(flops=0, bytes_accessed=4 * rowcount * width, transcendentals=0),
    )(jnp.stack([place["x"], place["core"]]), screened[0])

    pieces = pl.pallas_call(
        pieces_kernel,
        out_shape=jax.ShapeDtypeStruct((Z, sub, YH * nb), jnp.bfloat16),
        in_specs=[SMEM, SMEM, VMEM],
        out_specs=VMEM,
        scratch_shapes=[pltpu.VMEM((width, YH * nb), jnp.bfloat16)],
        compiler_params=PARAMS,
    )(place["yh"].reshape(1), jnp.concatenate([coef, their_coef]), both)
    got = lax.all_to_all(pieces, "z", 0, 0, tiled=True)
    rows = pl.pallas_call(
        rows_kernel,
        out_shape=jax.ShapeDtypeStruct((sub, mcols), jnp.bfloat16),
        in_specs=[VMEM],
        out_specs=VMEM,
        compiler_params=PARAMS,
    )(got)
    rows = lax.all_gather(rows, "yl", axis=0, tiled=True)
    blocks = []
    for step in range(X):
        block = rows if step == 0 else lax.ppermute(rows, "x", [(i, (i - step) % X) for i in range(X)])
        blocks += [block, lax.ppermute(block, "core", swap)]

    half = pl.pallas_call(
        half_kernel,
        grid=(rowcount // tile,),
        out_shape=jax.ShapeDtypeStruct((mcols, rowcount), jnp.bfloat16),
        in_specs=[
            pl.BlockSpec((mcols, width), lambda j: (0, 0)),
            pl.BlockSpec((tile, width), lambda j: (j, 0)),
        ],
        out_specs=pl.BlockSpec((mcols, tile), lambda j: (0, j)),
        compiler_params=PARAMS,
        cost_estimate=pl.CostEstimate(
            flops=2 * width * mcols * rowcount, bytes_accessed=10 << 20, transcendentals=0
        ),
    )(cols, ordered)
    part = pl.pallas_call(
        sigma_kernel,
        out_shape=jax.ShapeDtypeStruct((nb, nb), jnp.float32),
        in_specs=[VMEM] * (1 + len(blocks)),
        out_specs=VMEM,
        compiler_params=PARAMS,
        cost_estimate=pl.CostEstimate(
            flops=2 * rowcount * mcols * tile, bytes_accessed=6 << 20, transcendentals=0
        ),
    )(half, *blocks)

    share = nb // (Z * YH)
    part = lax.all_to_all(part.reshape(Z * YH, share, nb), BAND, 0, 0, tiled=True).sum(axis=0)
    spread = jnp.broadcast_to(part[None], (X * YL * CORE, share, nb))
    return lax.all_to_all(spread, GA, 0, 0, tiled=True).sum(axis=0)


def solution(mesh):
    fine = Mesh(mesh.devices.reshape(Z, YH, X, YL, CORE), BAND + GA)
    return jax.shard_map(
        on_device,
        mesh=fine,
        in_specs=(P(BAND, None, GA), P(BAND), P(), P(BAND, None, None, GA)),
        out_specs=P(BAND, None),
        check_vma=False,
    )
```

```python
import jax
import jax.numpy as jnp
from jax import lax
from jax.experimental import pallas as pl
from jax.experimental.pallas import tpu as pltpu
from jax.sharding import Mesh
from jax.sharding import PartitionSpec as P

NFREQ = 16
Z, YH, X, YL, CORE = 12, 2, 4, 4, 2
BAND = ("z", "yh")
GA = ("x", "yl", "core")
GROUP = 8
VMEM = pl.BlockSpec(memory_space=pltpu.VMEM)
SMEM = pl.BlockSpec(memory_space=pltpu.SMEM)
PARAMS = pltpu.CompilerParams(vmem_limit_bytes=16 << 20)


def turn_kernel(x_ref, core_ref, _, w_ref, out_ref):
    rows = [
        w_ref[(lax.rem(x_ref[0] + step, X) * YL + yl) * CORE + core]
        for step in range(X)
        for core in (core_ref[0], 1 - core_ref[0])
        for yl in range(YL)
    ]
    out_ref[...] = jnp.concatenate(rows, axis=0).T


def pieces_kernel(coef_ref, mine_ref, out_ref):
    count, depth, _ = out_ref.shape
    turned = (mine_ref[...].astype(jnp.float32) * coef_ref[0]).T
    for z in range(count):
        start = z * YH * depth
        halves = [turned[start + i * depth : start + (i + 1) * depth] for i in range(YH)]
        out_ref[z] = jnp.concatenate(halves, axis=1).astype(out_ref.dtype)


def split_kernel(yh_ref, got_ref, keep_ref, give_ref):
    nb = got_ref.shape[2] // YH
    pieces = [got_ref[z].astype(jnp.float32) for z in range(Z)]
    halves = [
        jnp.concatenate([p[:, i * nb : (i + 1) * nb] for p in pieces], axis=1) for i in range(YH)
    ]
    first = yh_ref[0] == 0
    keep_ref[...] = jnp.where(first, halves[0], halves[1]).astype(keep_ref.dtype)
    give_ref[...] = jnp.where(first, halves[1], halves[0]).astype(give_ref.dtype)


def join_kernel(keep_ref, came_ref, out_ref):
    parts = [keep_ref[...].astype(jnp.float32), came_ref[...].astype(jnp.float32)]
    out_ref[...] = jnp.concatenate(parts, axis=1).astype(out_ref.dtype)


def proj_kernel(wt_ref, *refs):
    row_refs, out_ref = refs[:-1], refs[-1]
    tile = GROUP * (out_ref.shape[1] // (Z * YH))
    for g in range(out_ref.shape[1] // tile):
        span = slice(g * tile, (g + 1) * tile)
        rows = jnp.concatenate([r[:, span] for r in row_refs], axis=0)
        out_ref[:, span] = jnp.dot(
            wt_ref[...], rows, preferred_element_type=jnp.float32
        ).astype(out_ref.dtype)


def sigma_kernel(cols_ref, proj_ref, out_ref, cols_buf, proj_buf, sems):
    nb = out_ref.shape[0]
    groups, _, _, width = cols_buf.shape
    tile = GROUP * nb
    copies = []
    for g in range(groups):
        parts = [(proj_ref.at[:, pl.ds(g * tile, tile)], proj_buf.at[g])]
        for side in range(YH):
            low, high = max(g * GROUP, side * Z), min((g + 1) * GROUP, (side + 1) * Z)
            if low < high:
                parts.append(
                    (
                        cols_ref.at[pl.ds(low - side * Z, high - low), side],
                        cols_buf.at[g, pl.ds(low - g * GROUP, high - low)],
                    )
                )
        copies.append([pltpu.make_async_copy(a, b, sems.at[g, i]) for i, (a, b) in enumerate(parts)])
    for copy in sum(copies, []):
        copy.start()
    sigma = jnp.zeros((nb, nb), jnp.float32)
    for g in range(groups):
        for copy in copies[g]:
            copy.wait()
        block = jnp.dot(
            cols_buf[g].reshape(tile, width), proj_buf[g], preferred_element_type=jnp.float32
        )
        for i in range(GROUP):
            sigma += block[i * nb : (i + 1) * nb, i * nb : (i + 1) * nb]
    out_ref[...] = sigma.T


def on_device(pair_dens, energies, freq_index, screened):
    mine = pair_dens[0]
    nb, width = mine.shape
    sub = width // (Z * YH)
    rowcount = X * YL * CORE * sub
    mcols = Z * YH * nb
    tile = GROUP * nb
    place = {axis: lax.axis_index(axis).astype(jnp.int32).reshape(1) for axis in ("yh", "x", "core")}
    swap = [(0, 1), (1, 0)]

    omega = 0.1 * jnp.exp(jnp.log(20.0) * freq_index[0].astype(jnp.float32) / (NFREQ - 1))
    coef = energies / (energies * energies + omega * omega)
    pieces = pl.pallas_call(
        pieces_kernel,
        out_shape=jax.ShapeDtypeStruct((Z, sub, YH * nb), jnp.bfloat16),
        in_specs=[SMEM, VMEM],
        out_specs=VMEM,
        compiler_params=PARAMS,
    )(coef, mine)
    got = lax.all_to_all(pieces, "z", 0, 0, tiled=True)

    theirs = lax.ppermute(mine, "yh", swap)
    both, got = lax.optimization_barrier((jnp.stack([mine, theirs]), got))
    cols = lax.all_gather(both, "z")

    keep, give = pl.pallas_call(
        split_kernel,
        out_shape=[jax.ShapeDtypeStruct((sub, Z * nb), jnp.bfloat16)] * 2,
        in_specs=[SMEM, VMEM],
        out_specs=[VMEM] * 2,
        compiler_params=PARAMS,
    )(place["yh"], got)
    turned = pl.pallas_call(
        turn_kernel,
        out_shape=jax.ShapeDtypeStruct((width, rowcount), jnp.bfloat16),
        in_specs=[SMEM, SMEM, pl.BlockSpec(memory_space=pl.ANY), VMEM],
        out_specs=VMEM,
        compiler_params=PARAMS,
        cost_estimate=pl.CostEstimate(flops=0, bytes_accessed=4 * rowcount * width, transcendentals=0),
    )(place["x"], place["core"], keep, screened[0])
    came, turned = lax.optimization_barrier((lax.ppermute(give, "yh", swap), turned))
    rows = pl.pallas_call(
        join_kernel,
        out_shape=jax.ShapeDtypeStruct((sub, mcols), jnp.bfloat16),
        in_specs=[VMEM] * 2,
        out_specs=VMEM,
        compiler_params=PARAMS,
    )(keep, came)
    rows = lax.all_gather(rows, "yl", axis=0, tiled=True)
    blocks = []
    for step in range(X):
        block = rows if step == 0 else lax.ppermute(rows, "x", [(i, (i - step) % X) for i in range(X)])
        blocks += [block, lax.ppermute(block, "core", swap)]

    proj = pl.pallas_call(
        proj_kernel,
        out_shape=jax.ShapeDtypeStruct((width, mcols), jnp.bfloat16),
        in_specs=[VMEM] * (1 + len(blocks)),
        out_specs=VMEM,
        compiler_params=PARAMS,
        cost_estimate=pl.CostEstimate(
            flops=2 * width * mcols * rowcount, bytes_accessed=10 << 20, transcendentals=0
        ),
    )(turned, *blocks)
    part = pl.pallas_call(
        sigma_kernel,
        out_shape=jax.ShapeDtypeStruct((nb, nb), jnp.float32),
        in_specs=[pl.BlockSpec(memory_space=pl.ANY)] * 2,
        out_specs=VMEM,
        scratch_shapes=[
            pltpu.VMEM((mcols // tile, GROUP, nb, width), jnp.bfloat16),
            pltpu.VMEM((mcols // tile, width, tile), jnp.bfloat16),
            pltpu.SemaphoreType.DMA((mcols // tile, 1 + YH)),
        ],
        compiler_params=pltpu.CompilerParams(vmem_limit_bytes=60 << 20),
        cost_estimate=pl.CostEstimate(
            flops=2 * width * mcols * tile, bytes_accessed=6 << 20, transcendentals=0
        ),
    )(cols, proj)

    share = nb // (Z * YH)
    part = lax.all_to_all(part.reshape(Z * YH, share, nb), BAND, 0, 0, tiled=True).sum(axis=0)
    spread = jnp.broadcast_to(part[None], (X * YL * CORE, share, nb))
    return lax.all_to_all(spread, GA, 0, 0, tiled=True).sum(axis=0)


def solution(mesh):
    fine = Mesh(mesh.devices.reshape(Z, YH, X, YL, CORE), BAND + GA)
    return jax.shard_map(
        on_device,
        mesh=fine,
        in_specs=(P(BAND, None, GA), P(BAND), P(), P(BAND, None, None, GA)),
        out_specs=P(BAND, None),
        check_vma=False,
    )
```

```python
import math

import jax
import jax.numpy as jnp
from jax import lax
from jax.experimental import pallas as pl
from jax.experimental.pallas import tpu as pltpu
from jax.sharding import Mesh
from jax.sharding import PartitionSpec as P

NFREQ = 16
Z, YH, X, YL, CORE = 12, 2, 4, 4, 2
BAND = ("z", "yh")
GA = ("x", "yl", "core")
GROUP = 8
VMEM = pl.BlockSpec(memory_space=pltpu.VMEM)
SMEM = pl.BlockSpec(memory_space=pltpu.SMEM)
PARAMS = pltpu.CompilerParams(vmem_limit_bytes=16 << 20)


def turn_kernel(x_ref, core_ref, _, w_ref, out_ref):
    rows = [
        w_ref[(lax.rem(x_ref[0] + step, X) * YL + yl) * CORE + core]
        for step in range(X)
        for core in (core_ref[0], 1 - core_ref[0])
        for yl in range(YL)
    ]
    out_ref[...] = jnp.concatenate(rows, axis=0).T


def label_kernel(energy_ref, mine_ref, out_ref):
    nb, width = mine_ref.shape
    out_ref[:nb, :] = mine_ref[...]
    shape = (out_ref.shape[0] - nb, width)
    energy = jnp.full(shape, energy_ref[0], jnp.float32)
    high = energy.astype(jnp.bfloat16).astype(jnp.float32)
    middle = (energy - high).astype(jnp.bfloat16).astype(jnp.float32)
    low = energy - high - middle
    lane = lax.broadcasted_iota(jnp.int32, shape, 1)
    parts = jnp.where(lane == 0, high, jnp.where(lane == 1, middle, low))
    kept = (lane < 3) & (lax.broadcasted_iota(jnp.int32, shape, 0) == 0)
    out_ref[nb:, :] = jnp.where(kept, parts, 0.0).astype(out_ref.dtype)


def pieces_kernel(yh_ref, freq_ref, both_ref, out_ref, turned_ref):
    sub = out_ref.shape[1]
    nb = out_ref.shape[2] // YH
    step = jnp.full((1, 128), freq_ref[0], jnp.int32).astype(jnp.float32)
    omega = 0.1 * jnp.exp(math.log(20.0) * step / (NFREQ - 1))
    scaled = []
    for i in range(YH):
        label = both_ref[i, nb:, :128].astype(jnp.float32)
        energy = jnp.sum(jnp.sum(label, axis=1, keepdims=True), axis=0, keepdims=True)
        coef = energy / (energy * energy + omega * omega)
        scaled.append(both_ref[i, :nb, :].astype(jnp.float32) * coef[:, :1])
    turned_ref[...] = jnp.concatenate(scaled, axis=0).T.astype(turned_ref.dtype)
    for z in range(Z):
        start = pl.multiple_of((z * YH + yh_ref[0]) * sub, sub)
        out_ref[z] = turned_ref[pl.ds(start, sub), :]


def rows_kernel(got_ref, out_ref):
    out_ref[...] = jnp.concatenate([got_ref[z] for z in range(Z)], axis=1)


def proj_kernel(wt_ref, *refs):
    row_refs, out_ref = refs[:-1], refs[-1]
    tile = GROUP * (out_ref.shape[1] // (Z * YH))
    for g in range(out_ref.shape[1] // tile):
        span = slice(g * tile, (g + 1) * tile)
        rows = jnp.concatenate([r[:, span] for r in row_refs], axis=0)
        out_ref[:, span] = jnp.dot(
            wt_ref[...], rows, preferred_element_type=jnp.float32
        ).astype(out_ref.dtype)


def sigma_kernel(cols_ref, proj_ref, out_ref, cols_buf, proj_buf, sems):
    groups, count, sides, nb, width = cols_buf.shape
    tile = count * sides * nb
    copies = [
        (
            pltpu.make_async_copy(
                cols_ref.at[pl.ds(g * count, count), :, pl.ds(0, nb)], cols_buf.at[g], sems.at[g, 0]
            ),
            pltpu.make_async_copy(proj_ref.at[:, pl.ds(g * tile, tile)], proj_buf.at[g], sems.at[g, 1]),
        )
        for g in range(groups)
    ]
    for copy in sum(copies, ()):
        copy.start()
    sigma = jnp.zeros((nb, nb), jnp.float32)
    for g in range(groups):
        for copy in copies[g]:
            copy.wait()
        block = jnp.dot(
            cols_buf[g].reshape(tile, width), proj_buf[g], preferred_element_type=jnp.float32
        )
        for i in range(GROUP):
            sigma += block[i * nb : (i + 1) * nb, i * nb : (i + 1) * nb]
    out_ref[...] = sigma.T


def on_device(pair_dens, energies, freq_index, screened):
    mine = pair_dens[0]
    nb, width = mine.shape
    sub = width // (Z * YH)
    rowcount = X * YL * CORE * sub
    mcols = Z * YH * nb
    tile = GROUP * nb
    place = {axis: lax.axis_index(axis).astype(jnp.int32).reshape(1) for axis in ("yh", "x", "core")}
    swap = [(0, 1), (1, 0)]

    labelled = pl.pallas_call(
        label_kernel,
        out_shape=jax.ShapeDtypeStruct((nb + 8, width), jnp.bfloat16),
        in_specs=[SMEM, VMEM],
        out_specs=VMEM,
        compiler_params=PARAMS,
    )(energies, mine)
    both = lax.optimization_barrier(lax.all_gather(labelled, "yh"))
    cols = lax.all_gather(both, "z")

    pieces = pl.pallas_call(
        pieces_kernel,
        out_shape=jax.ShapeDtypeStruct((Z, sub, YH * nb), jnp.bfloat16),
        in_specs=[SMEM, SMEM, VMEM],
        out_specs=VMEM,
        scratch_shapes=[pltpu.VMEM((width, YH * nb), jnp.bfloat16)],
        compiler_params=PARAMS,
    )(place["yh"], freq_index, both)
    got = lax.all_to_all(pieces, "z", 0, 0, tiled=True)
    rows = pl.pallas_call(
        rows_kernel,
        out_shape=jax.ShapeDtypeStruct((sub, mcols), jnp.bfloat16),
        in_specs=[VMEM],
        out_specs=VMEM,
        compiler_params=PARAMS,
    )(got)
    rows = lax.all_gather(rows, "yl", axis=0, tiled=True)
    turned = pl.pallas_call(
        turn_kernel,
        out_shape=jax.ShapeDtypeStruct((width, rowcount), jnp.bfloat16),
        in_specs=[SMEM, SMEM, pl.BlockSpec(memory_space=pl.ANY), VMEM],
        out_specs=VMEM,
        compiler_params=PARAMS,
        cost_estimate=pl.CostEstimate(flops=0, bytes_accessed=4 * rowcount * width, transcendentals=0),
    )(place["x"], place["core"], rows, screened[0])
    further = [
        lax.ppermute(rows, "x", [(i, (i - step) % X) for i in range(X)]) for step in range(1, X)
    ]
    further[0], turned = lax.optimization_barrier((further[0], turned))
    blocks = []
    for block in [rows] + further:
        blocks += [block, lax.ppermute(block, "core", swap)]

    proj = pl.pallas_call(
        proj_kernel,
        out_shape=jax.ShapeDtypeStruct((width, mcols), jnp.bfloat16),
        in_specs=[VMEM] * (1 + len(blocks)),
        out_specs=VMEM,
        compiler_params=PARAMS,
        cost_estimate=pl.CostEstimate(
            flops=2 * width * mcols * rowcount, bytes_accessed=10 << 20, transcendentals=0
        ),
    )(turned, *blocks)
    part = pl.pallas_call(
        sigma_kernel,
        out_shape=jax.ShapeDtypeStruct((nb, nb), jnp.float32),
        in_specs=[pl.BlockSpec(memory_space=pl.ANY)] * 2,
        out_specs=VMEM,
        scratch_shapes=[
            pltpu.VMEM((mcols // tile, GROUP // YH, YH, nb, width), jnp.bfloat16),
            pltpu.VMEM((mcols // tile, width, tile), jnp.bfloat16),
            pltpu.SemaphoreType.DMA((mcols // tile, 2)),
        ],
        compiler_params=pltpu.CompilerParams(vmem_limit_bytes=60 << 20),
        cost_estimate=pl.CostEstimate(
            flops=2 * width * mcols * tile, bytes_accessed=6 << 20, transcendentals=0
        ),
    )(cols, proj)

    share = nb // (Z * YH)
    part = lax.all_to_all(part.reshape(Z * YH, share, nb), BAND, 0, 0, tiled=True).sum(axis=0)
    spread = jnp.broadcast_to(part[None], (X * YL * CORE, share, nb))
    return lax.all_to_all(spread, GA, 0, 0, tiled=True).sum(axis=0)


def solution(mesh):
    fine = Mesh(mesh.devices.reshape(Z, YH, X, YL, CORE), BAND + GA)
    return jax.shard_map(
        on_device,
        mesh=fine,
        in_specs=(P(BAND, None, GA), P(BAND), P(), P(BAND, None, None, GA)),
        out_specs=P(BAND, None),
        check_vma=False,
    )
```

```python
import math

import jax
import jax.numpy as jnp
from jax import lax
from jax.experimental import pallas as pl
from jax.experimental.pallas import tpu as pltpu
from jax.sharding import Mesh
from jax.sharding import PartitionSpec as P

NFREQ = 16
Z, YH, X, YL, CORE = 12, 2, 4, 4, 2
BAND = ("z", "yh")
GA = ("x", "yl", "core")
GROUP = 8
SPANS = [slice(i, min(i + 256, 1152)) for i in range(0, 1152, 256)]
VMEM = pl.BlockSpec(memory_space=pltpu.VMEM)
SMEM = pl.BlockSpec(memory_space=pltpu.SMEM)
PARAMS = pltpu.CompilerParams(vmem_limit_bytes=16 << 20)


def turn_kernel(x_ref, core_ref, _, w_ref, out_ref):
    rows = [
        w_ref[(lax.rem(x_ref[0] + step, X) * YL + yl) * CORE + core]
        for step in range(X)
        for core in (core_ref[0], 1 - core_ref[0])
        for yl in range(YL)
    ]
    out_ref[...] = jnp.concatenate(rows, axis=0).T


def label_kernel(energy_ref, mine_ref, out_ref):
    nb, width = mine_ref.shape
    out_ref[:nb, :] = mine_ref[...]
    shape = (out_ref.shape[0] - nb, width)
    energy = jnp.full(shape, energy_ref[0], jnp.float32)
    high = energy.astype(jnp.bfloat16).astype(jnp.float32)
    middle = (energy - high).astype(jnp.bfloat16).astype(jnp.float32)
    low = energy - high - middle
    lane = lax.broadcasted_iota(jnp.int32, shape, 1)
    parts = jnp.where(lane == 0, high, jnp.where(lane == 1, middle, low))
    kept = (lane < 3) & (lax.broadcasted_iota(jnp.int32, shape, 0) == 0)
    out_ref[nb:, :] = jnp.where(kept, parts, 0.0).astype(out_ref.dtype)


def pieces_kernel(yh_ref, freq_ref, both_ref, out_ref, turned_ref):
    sub = out_ref.shape[1]
    nb = out_ref.shape[2] // YH
    step = jnp.full((1, 128), freq_ref[0], jnp.int32).astype(jnp.float32)
    omega = 0.1 * jnp.exp(math.log(20.0) * step / (NFREQ - 1))
    scaled = []
    for i in range(YH):
        label = both_ref[i, nb:, :128].astype(jnp.float32)
        energy = jnp.sum(jnp.sum(label, axis=1, keepdims=True), axis=0, keepdims=True)
        coef = energy / (energy * energy + omega * omega)
        scaled.append(both_ref[i, :nb, :].astype(jnp.float32) * coef[:, :1])
    turned_ref[...] = jnp.concatenate(scaled, axis=0).T.astype(turned_ref.dtype)
    for z in range(Z):
        start = pl.multiple_of((z * YH + yh_ref[0]) * sub, sub)
        out_ref[z] = turned_ref[pl.ds(start, sub), :]


def rows_kernel(got_ref, out_ref):
    out_ref[...] = jnp.concatenate([got_ref[z] for z in range(Z)], axis=1)


def proj_kernel(wt_ref, *refs):
    row_refs, out_ref = refs[:-1], refs[-1]
    for span in SPANS:
        rows = jnp.concatenate([r[:, span] for r in row_refs], axis=0)
        out_ref[:, span] = jnp.dot(
            wt_ref[...], rows, preferred_element_type=jnp.float32
        ).astype(out_ref.dtype)


def sigma_kernel(cols_ref, proj_ref, out_ref, cols_buf, proj_buf, sems):
    groups, count, sides, nb, width = cols_buf.shape
    tile = count * sides * nb
    copies = [
        (
            pltpu.make_async_copy(
                cols_ref.at[pl.ds(g * count, count), :, pl.ds(0, nb)], cols_buf.at[g], sems.at[g, 0]
            ),
            pltpu.make_async_copy(proj_ref.at[:, pl.ds(g * tile, tile)], proj_buf.at[g], sems.at[g, 1]),
        )
        for g in range(groups)
    ]
    for copy in sum(copies, ()):
        copy.start()
    sigma = jnp.zeros((nb, nb), jnp.float32)
    for g in range(groups):
        for copy in copies[g]:
            copy.wait()
        block = jnp.dot(
            cols_buf[g].reshape(tile, width), proj_buf[g], preferred_element_type=jnp.float32
        )
        for i in range(GROUP):
            sigma += block[i * nb : (i + 1) * nb, i * nb : (i + 1) * nb]
    out_ref[...] = sigma.T


def on_device(pair_dens, energies, freq_index, screened):
    mine = pair_dens[0]
    nb, width = mine.shape
    sub = width // (Z * YH)
    rowcount = X * YL * CORE * sub
    mcols = Z * YH * nb
    tile = GROUP * nb
    place = {axis: lax.axis_index(axis).astype(jnp.int32).reshape(1) for axis in ("yh", "x", "core")}
    swap = [(0, 1), (1, 0)]

    labelled = pl.pallas_call(
        label_kernel,
        out_shape=jax.ShapeDtypeStruct((nb + 8, width), jnp.bfloat16),
        in_specs=[SMEM, VMEM],
        out_specs=VMEM,
        compiler_params=PARAMS,
    )(energies, mine)
    both = lax.optimization_barrier(lax.all_gather(labelled, "yh"))
    cols = lax.all_gather(both, "z")

    pieces = pl.pallas_call(
        pieces_kernel,
        out_shape=jax.ShapeDtypeStruct((Z, sub, YH * nb), jnp.bfloat16),
        in_specs=[SMEM, SMEM, VMEM],
        out_specs=VMEM,
        scratch_shapes=[pltpu.VMEM((width, YH * nb), jnp.bfloat16)],
        compiler_params=PARAMS,
    )(place["yh"], freq_index, both)
    got = lax.all_to_all(pieces, "z", 0, 0, tiled=True)
    rows = pl.pallas_call(
        rows_kernel,
        out_shape=jax.ShapeDtypeStruct((sub, mcols), jnp.bfloat16),
        in_specs=[VMEM],
        out_specs=VMEM,
        compiler_params=PARAMS,
    )(got)
    rows = lax.all_gather(rows, "yl", axis=0, tiled=True)
    turned = pl.pallas_call(
        turn_kernel,
        out_shape=jax.ShapeDtypeStruct((width, rowcount), jnp.bfloat16),
        in_specs=[SMEM, SMEM, pl.BlockSpec(memory_space=pl.ANY), VMEM],
        out_specs=VMEM,
        compiler_params=PARAMS,
        cost_estimate=pl.CostEstimate(flops=0, bytes_accessed=4 * rowcount * width, transcendentals=0),
    )(place["x"], place["core"], rows, screened[0])
    further = [
        lax.ppermute(rows, "x", [(i, (i - step) % X) for i in range(X)]) for step in range(1, X)
    ]
    further[0], turned = lax.optimization_barrier((further[0], turned))
    blocks = []
    for block in [rows] + further:
        blocks += [block, lax.ppermute(block, "core", swap)]

    proj = pl.pallas_call(
        proj_kernel,
        out_shape=jax.ShapeDtypeStruct((width, mcols), jnp.bfloat16),
        in_specs=[VMEM] * (1 + len(blocks)),
        out_specs=VMEM,
        compiler_params=PARAMS,
        cost_estimate=pl.CostEstimate(
            flops=2 * width * mcols * rowcount, bytes_accessed=10 << 20, transcendentals=0
        ),
    )(turned, *blocks)
    part = pl.pallas_call(
        sigma_kernel,
        out_shape=jax.ShapeDtypeStruct((nb, nb), jnp.float32),
        in_specs=[pl.BlockSpec(memory_space=pl.ANY)] * 2,
        out_specs=VMEM,
        scratch_shapes=[
            pltpu.VMEM((mcols // tile, GROUP // YH, YH, nb, width), jnp.bfloat16),
            pltpu.VMEM((mcols // tile, width, tile), jnp.bfloat16),
            pltpu.SemaphoreType.DMA((mcols // tile, 2)),
        ],
        compiler_params=pltpu.CompilerParams(vmem_limit_bytes=60 << 20),
        cost_estimate=pl.CostEstimate(
            flops=2 * width * mcols * tile, bytes_accessed=6 << 20, transcendentals=0
        ),
    )(cols, proj)

    share = nb // (Z * YH)
    part = lax.all_to_all(part.reshape(Z * YH, share, nb), BAND, 0, 0, tiled=True).sum(axis=0)
    spread = jnp.broadcast_to(part[None], (X * YL * CORE, share, nb))
    return lax.all_to_all(spread, GA, 0, 0, tiled=True).sum(axis=0)


def solution(mesh):
    fine = Mesh(mesh.devices.reshape(Z, YH, X, YL, CORE), BAND + GA)
    return jax.shard_map(
        on_device,
        mesh=fine,
        in_specs=(P(BAND, None, GA), P(BAND), P(), P(BAND, None, None, GA)),
        out_specs=P(BAND, None),
        check_vma=False,
    )
```

```python
import math

import jax
import jax.numpy as jnp
from jax import lax
from jax.experimental import pallas as pl
from jax.experimental.pallas import tpu as pltpu
from jax.sharding import Mesh
from jax.sharding import PartitionSpec as P

NFREQ = 16
Z, YH, X, YL, CORE = 12, 2, 4, 4, 2
BAND = ("z", "yh")
GA = ("x", "yl", "core")
GROUP = 8
SPANS = [slice(i, min(i + 256, 1152)) for i in range(0, 1152, 256)]
VMEM = pl.BlockSpec(memory_space=pltpu.VMEM)
SMEM = pl.BlockSpec(memory_space=pltpu.SMEM)
PARAMS = pltpu.CompilerParams(vmem_limit_bytes=16 << 20)


def turn_kernel(x_ref, core_ref, _, w_ref, out_ref):
    rows = [
        w_ref[(lax.rem(x_ref[0] + step, X) * YL + yl) * CORE + core]
        for step in range(X)
        for core in ((core_ref[0], 1 - core_ref[0]) if step < X - 1 else range(CORE))
        for yl in range(YL)
    ]
    out_ref[...] = jnp.concatenate(rows, axis=0).T


def label_kernel(energy_ref, mine_ref, out_ref):
    nb, width = mine_ref.shape
    out_ref[:nb, :] = mine_ref[...]
    shape = (out_ref.shape[0] - nb, width)
    energy = jnp.full(shape, energy_ref[0], jnp.float32)
    high = energy.astype(jnp.bfloat16).astype(jnp.float32)
    middle = (energy - high).astype(jnp.bfloat16).astype(jnp.float32)
    low = energy - high - middle
    lane = lax.broadcasted_iota(jnp.int32, shape, 1)
    parts = jnp.where(lane == 0, high, jnp.where(lane == 1, middle, low))
    kept = (lane < 3) & (lax.broadcasted_iota(jnp.int32, shape, 0) == 0)
    out_ref[nb:, :] = jnp.where(kept, parts, 0.0).astype(out_ref.dtype)


def pieces_kernel(yh_ref, freq_ref, both_ref, out_ref, turned_ref):
    sub = out_ref.shape[1]
    nb = out_ref.shape[2] // YH
    step = jnp.full((1, 128), freq_ref[0], jnp.int32).astype(jnp.float32)
    omega = 0.1 * jnp.exp(math.log(20.0) * step / (NFREQ - 1))
    scaled = []
    for i in range(YH):
        label = both_ref[i, nb:, :128].astype(jnp.float32)
        energy = jnp.sum(jnp.sum(label, axis=1, keepdims=True), axis=0, keepdims=True)
        coef = energy / (energy * energy + omega * omega)
        scaled.append(both_ref[i, :nb, :].astype(jnp.float32) * coef[:, :1])
    turned_ref[...] = jnp.concatenate(scaled, axis=0).T.astype(turned_ref.dtype)
    for z in range(Z):
        start = pl.multiple_of((z * YH + yh_ref[0]) * sub, sub)
        out_ref[z] = turned_ref[pl.ds(start, sub), :]


def rows_kernel(got_ref, out_ref):
    out_ref[...] = jnp.concatenate([got_ref[z] for z in range(Z)], axis=1)


def proj_kernel(wt_ref, *refs):
    row_refs, out_ref = refs[:-1], refs[-1]
    for span in SPANS:
        rows = jnp.concatenate([r[:, span] for r in row_refs], axis=0)
        out_ref[:, span] = jnp.dot(
            wt_ref[...], rows, preferred_element_type=jnp.float32
        ).astype(out_ref.dtype)


def sigma_kernel(cols_ref, proj_ref, out_ref, cols_buf, proj_buf, sems):
    groups, count, sides, nb, width = cols_buf.shape
    tile = count * sides * nb
    copies = [
        (
            pltpu.make_async_copy(
                cols_ref.at[pl.ds(g * count, count), :, pl.ds(0, nb)], cols_buf.at[g], sems.at[g, 0]
            ),
            pltpu.make_async_copy(proj_ref.at[:, pl.ds(g * tile, tile)], proj_buf.at[g], sems.at[g, 1]),
        )
        for g in range(groups)
    ]
    for copy in sum(copies, ()):
        copy.start()
    sigma = jnp.zeros((nb, nb), jnp.float32)
    for g in range(groups):
        for copy in copies[g]:
            copy.wait()
        block = jnp.dot(
            cols_buf[g].reshape(tile, width), proj_buf[g], preferred_element_type=jnp.float32
        )
        for i in range(GROUP):
            sigma += block[i * nb : (i + 1) * nb, i * nb : (i + 1) * nb]
    out_ref[...] = sigma.T


def on_device(pair_dens, energies, freq_index, screened):
    mine = pair_dens[0]
    nb, width = mine.shape
    sub = width // (Z * YH)
    rowcount = X * YL * CORE * sub
    mcols = Z * YH * nb
    tile = GROUP * nb
    place = {axis: lax.axis_index(axis).astype(jnp.int32).reshape(1) for axis in ("yh", "x", "core")}
    swap = [(0, 1), (1, 0)]

    labelled = pl.pallas_call(
        label_kernel,
        out_shape=jax.ShapeDtypeStruct((nb + 8, width), jnp.bfloat16),
        in_specs=[SMEM, VMEM],
        out_specs=VMEM,
        compiler_params=PARAMS,
    )(energies, mine)
    both = lax.optimization_barrier(lax.all_gather(labelled, "yh"))
    cols = lax.all_gather(both, "z")

    pieces = pl.pallas_call(
        pieces_kernel,
        out_shape=jax.ShapeDtypeStruct((Z, sub, YH * nb), jnp.bfloat16),
        in_specs=[SMEM, SMEM, VMEM],
        out_specs=VMEM,
        scratch_shapes=[pltpu.VMEM((width, YH * nb), jnp.bfloat16)],
        compiler_params=PARAMS,
    )(place["yh"], freq_index, both)
    got = lax.all_to_all(pieces, "z", 0, 0, tiled=True)
    rows = pl.pallas_call(
        rows_kernel,
        out_shape=jax.ShapeDtypeStruct((sub, mcols), jnp.bfloat16),
        in_specs=[VMEM],
        out_specs=VMEM,
        compiler_params=PARAMS,
    )(got)
    rows = lax.all_gather(rows, "yl", axis=0, tiled=True)
    turned = pl.pallas_call(
        turn_kernel,
        out_shape=jax.ShapeDtypeStruct((width, rowcount), jnp.bfloat16),
        in_specs=[SMEM, SMEM, pl.BlockSpec(memory_space=pl.ANY), VMEM],
        out_specs=VMEM,
        compiler_params=PARAMS,
        cost_estimate=pl.CostEstimate(flops=0, bytes_accessed=4 * rowcount * width, transcendentals=0),
    )(place["x"], place["core"], rows, screened[0])
    further = [
        lax.ppermute(rows, "x", [(i, (i - step) % X) for i in range(X)]) for step in range(1, X)
    ]
    further[0], turned = lax.optimization_barrier((further[0], turned))
    blocks = []
    for block in [rows] + further[:-1]:
        blocks += [block, lax.ppermute(block, "core", swap)]
    blocks.append(lax.all_gather(further[-1], "core", axis=0, tiled=True))

    proj = pl.pallas_call(
        proj_kernel,
        out_shape=jax.ShapeDtypeStruct((width, mcols), jnp.bfloat16),
        in_specs=[VMEM] * (1 + len(blocks)),
        out_specs=VMEM,
        compiler_params=PARAMS,
        cost_estimate=pl.CostEstimate(
            flops=2 * width * mcols * rowcount, bytes_accessed=10 << 20, transcendentals=0
        ),
    )(turned, *blocks)
    part = pl.pallas_call(
        sigma_kernel,
        out_shape=jax.ShapeDtypeStruct((nb, nb), jnp.float32),
        in_specs=[pl.BlockSpec(memory_space=pl.ANY)] * 2,
        out_specs=VMEM,
        scratch_shapes=[
            pltpu.VMEM((mcols // tile, GROUP // YH, YH, nb, width), jnp.bfloat16),
            pltpu.VMEM((mcols // tile, width, tile), jnp.bfloat16),
            pltpu.SemaphoreType.DMA((mcols // tile, 2)),
        ],
        compiler_params=pltpu.CompilerParams(vmem_limit_bytes=60 << 20),
        cost_estimate=pl.CostEstimate(
            flops=2 * width * mcols * tile, bytes_accessed=6 << 20, transcendentals=0
        ),
    )(cols, proj)

    share = nb // (Z * YH)
    part = lax.all_to_all(part.reshape(Z * YH, share, nb), BAND, 0, 0, tiled=True).sum(axis=0)
    spread = jnp.broadcast_to(part[None], (X * YL * CORE, share, nb))
    return lax.all_to_all(spread, GA, 0, 0, tiled=True).sum(axis=0)


def solution(mesh):
    fine = Mesh(mesh.devices.reshape(Z, YH, X, YL, CORE), BAND + GA)
    return jax.shard_map(
        on_device,
        mesh=fine,
        in_specs=(P(BAND, None, GA), P(BAND), P(), P(BAND, None, None, GA)),
        out_specs=P(BAND, None),
        check_vma=False,
    )
```

```python
import math

import jax
import jax.numpy as jnp
from jax import lax
from jax.experimental import pallas as pl
from jax.experimental.pallas import tpu as pltpu
from jax.sharding import Mesh
from jax.sharding import PartitionSpec as P

NFREQ = 16
Z, YH, X, YL, CORE = 12, 2, 4, 4, 2
BAND = ("z", "yh")
GA = ("x", "yl", "core")
GROUP = 8
SPANS = [slice(i, min(i + 256, 1152)) for i in range(0, 1152, 256)]
VMEM = pl.BlockSpec(memory_space=pltpu.VMEM)
SMEM = pl.BlockSpec(memory_space=pltpu.SMEM)
PARAMS = pltpu.CompilerParams(vmem_limit_bytes=16 << 20)


def turn_kernel(x_ref, core_ref, _, w_ref, out_ref):
    rows = [
        w_ref[(lax.rem(x_ref[0] + step, X) * YL + yl) * CORE + core]
        for step in range(X)
        for core in ((core_ref[0], 1 - core_ref[0]) if step < X - 1 else range(CORE))
        for yl in range(YL)
    ]
    out_ref[...] = jnp.concatenate(rows, axis=0).T


def label_kernel(energy_ref, mine_ref, out_ref):
    nb, width = mine_ref.shape
    out_ref[:nb, :] = mine_ref[...]
    shape = (out_ref.shape[0] - nb, width)
    energy = jnp.full(shape, energy_ref[0], jnp.float32)
    high = energy.astype(jnp.bfloat16).astype(jnp.float32)
    middle = (energy - high).astype(jnp.bfloat16).astype(jnp.float32)
    low = energy - high - middle
    lane = lax.broadcasted_iota(jnp.int32, shape, 1)
    parts = jnp.where(lane == 0, high, jnp.where(lane == 1, middle, low))
    kept = (lane < 3) & (lax.broadcasted_iota(jnp.int32, shape, 0) == 0)
    out_ref[nb:, :] = jnp.where(kept, parts, 0.0).astype(out_ref.dtype)


def pieces_kernel(yh_ref, freq_ref, both_ref, out_ref, turned_ref):
    sub = out_ref.shape[1]
    nb = out_ref.shape[2] // YH
    step = jnp.full((1, 128), freq_ref[0], jnp.int32).astype(jnp.float32)
    omega = 0.1 * jnp.exp(math.log(20.0) * step / (NFREQ - 1))
    scaled = []
    for i in range(YH):
        label = both_ref[i, nb:, :128].astype(jnp.float32)
        energy = jnp.sum(jnp.sum(label, axis=1, keepdims=True), axis=0, keepdims=True)
        coef = energy / (energy * energy + omega * omega)
        scaled.append(both_ref[i, :nb, :].astype(jnp.float32) * coef[:, :1])
    turned_ref[...] = jnp.concatenate(scaled, axis=0).T.astype(turned_ref.dtype)
    for z in range(Z):
        start = pl.multiple_of((z * YH + yh_ref[0]) * sub, sub)
        out_ref[z] = turned_ref[pl.ds(start, sub), :]


def rows_kernel(got_ref, out_ref):
    out_ref[...] = jnp.concatenate([got_ref[z] for z in range(Z)], axis=1)


def proj_kernel(wt_ref, *refs):
    row_refs, out_ref = refs[:-1], refs[-1]
    for span in SPANS:
        rows = jnp.concatenate([r[:, span] for r in row_refs], axis=0)
        out_ref[:, span] = jnp.dot(
            wt_ref[...], rows, preferred_element_type=jnp.float32
        ).astype(out_ref.dtype)


def sigma_kernel(cols_ref, proj_ref, out_ref, cols_buf, proj_buf, sems):
    groups, count, sides, nb, width = cols_buf.shape
    tile = count * sides * nb
    copies = [
        (
            pltpu.make_async_copy(
                cols_ref.at[pl.ds(g * count, count), :, pl.ds(0, nb)], cols_buf.at[g], sems.at[g, 0]
            ),
            pltpu.make_async_copy(proj_ref.at[:, pl.ds(g * tile, tile)], proj_buf.at[g], sems.at[g, 1]),
        )
        for g in range(groups)
    ]
    for copy in sum(copies, ()):
        copy.start()
    sigma = jnp.zeros((nb, nb), jnp.float32)
    for g in range(groups):
        for copy in copies[g]:
            copy.wait()
        block = jnp.dot(
            cols_buf[g].reshape(tile, width), proj_buf[g], preferred_element_type=jnp.float32
        )
        for i in range(GROUP):
            sigma += block[i * nb : (i + 1) * nb, i * nb : (i + 1) * nb]
    total = sigma.T
    share = out_ref.shape[1]
    for place in range(out_ref.shape[0]):
        start = place // CORE * share
        out_ref[place] = total[start : start + share]


def on_device(pair_dens, energies, freq_index, screened):
    mine = pair_dens[0]
    nb, width = mine.shape
    sub = width // (Z * YH)
    rowcount = X * YL * CORE * sub
    mcols = Z * YH * nb
    tile = GROUP * nb
    place = {axis: lax.axis_index(axis).astype(jnp.int32).reshape(1) for axis in ("yh", "x", "core")}
    swap = [(0, 1), (1, 0)]

    labelled = pl.pallas_call(
        label_kernel,
        out_shape=jax.ShapeDtypeStruct((nb + 8, width), jnp.bfloat16),
        in_specs=[SMEM, VMEM],
        out_specs=VMEM,
        compiler_params=PARAMS,
    )(energies, mine)
    both = lax.optimization_barrier(lax.all_gather(labelled, "yh"))
    cols = lax.all_gather(both, "z")

    pieces = pl.pallas_call(
        pieces_kernel,
        out_shape=jax.ShapeDtypeStruct((Z, sub, YH * nb), jnp.bfloat16),
        in_specs=[SMEM, SMEM, VMEM],
        out_specs=VMEM,
        scratch_shapes=[pltpu.VMEM((width, YH * nb), jnp.bfloat16)],
        compiler_params=PARAMS,
    )(place["yh"], freq_index, both)
    got = lax.all_to_all(pieces, "z", 0, 0, tiled=True)
    rows = pl.pallas_call(
        rows_kernel,
        out_shape=jax.ShapeDtypeStruct((sub, mcols), jnp.bfloat16),
        in_specs=[VMEM],
        out_specs=VMEM,
        compiler_params=PARAMS,
    )(got)
    rows = lax.all_gather(rows, "yl", axis=0, tiled=True)
    turned = pl.pallas_call(
        turn_kernel,
        out_shape=jax.ShapeDtypeStruct((width, rowcount), jnp.bfloat16),
        in_specs=[SMEM, SMEM, pl.BlockSpec(memory_space=pl.ANY), VMEM],
        out_specs=VMEM,
        compiler_params=PARAMS,
        cost_estimate=pl.CostEstimate(flops=0, bytes_accessed=4 * rowcount * width, transcendentals=0),
    )(place["x"], place["core"], rows, screened[0])
    further = [
        lax.ppermute(rows, "x", [(i, (i - step) % X) for i in range(X)]) for step in range(1, X)
    ]
    further[0], turned = lax.optimization_barrier((further[0], turned))
    blocks = []
    for block in [rows] + further[:-1]:
        blocks += [block, lax.ppermute(block, "core", swap)]
    blocks.append(lax.all_gather(further[-1], "core", axis=0, tiled=True))

    proj = pl.pallas_call(
        proj_kernel,
        out_shape=jax.ShapeDtypeStruct((width, mcols), jnp.bfloat16),
        in_specs=[VMEM] * (1 + len(blocks)),
        out_specs=VMEM,
        compiler_params=PARAMS,
        cost_estimate=pl.CostEstimate(
            flops=2 * width * mcols * rowcount, bytes_accessed=10 << 20, transcendentals=0
        ),
    )(turned, *blocks)
    share = nb // (Z * YH)
    part = pl.pallas_call(
        sigma_kernel,
        out_shape=jax.ShapeDtypeStruct((Z * YH * CORE, share, nb), jnp.float32),
        in_specs=[pl.BlockSpec(memory_space=pl.ANY)] * 2,
        out_specs=VMEM,
        scratch_shapes=[
            pltpu.VMEM((mcols // tile, GROUP // YH, YH, nb, width), jnp.bfloat16),
            pltpu.VMEM((mcols // tile, width, tile), jnp.bfloat16),
            pltpu.SemaphoreType.DMA((mcols // tile, 2)),
        ],
        compiler_params=pltpu.CompilerParams(vmem_limit_bytes=60 << 20),
        cost_estimate=pl.CostEstimate(
            flops=2 * width * mcols * tile, bytes_accessed=6 << 20, transcendentals=0
        ),
    )(cols, proj)

    part = lax.all_to_all(part, BAND + ("core",), 0, 0, tiled=True).sum(axis=0)
    spread = jnp.broadcast_to(part[None], (X * YL, share, nb))
    return lax.all_to_all(spread, ("x", "yl"), 0, 0, tiled=True).sum(axis=0)


def solution(mesh):
    fine = Mesh(mesh.devices.reshape(Z, YH, X, YL, CORE), BAND + GA)
    return jax.shard_map(
        on_device,
        mesh=fine,
        in_specs=(P(BAND, None, GA), P(BAND), P(), P(BAND, None, None, GA)),
        out_specs=P(BAND, None),
        check_vma=False,
    )
```
